32 devices in a mesh: clus: 4 (over y, x), wide: 8 (over z, core).
Axes of the slice: x: 2, y: 2, z: 4, core: 2. Of those that a mesh axis runs over, the one named last changes fastest.
Arguments:
- documents: bfloat16 [16384, 768], P(('clus', 'wide')), may hold values from -96 to 96
- source_device: int32 [4, 4096], P('clus', 'wide'), may hold values from 0 to 31, as said below
- source_row: int32 [4, 4096], P('clus', 'wide'), may hold values from 0 to 511
- centroids: float32 [4, 768], P('clus'), may hold values from -6 to 6
Outputs:
- nearest_earlier: float32 [4, 4096], P('clus', 'wide')
- centroid_distance: float32 [4, 4096], P('clus', 'wide')
The draws below stay inside these ranges and needn't reach their ends.
Inputs may be any that keep to these rules, and one draw needn't show every extreme that they name: Together, (source_device, source_row) name every document row exactly once over all clusters. Among the 512 members of one device's block (members w * 512 to (w + 1) * 512 - 1 of a cluster) at most 32 come from one source device, and in every such block some source device supplies exactly 32.
All inputs are finite; a program needn't handle non-finite values.
Results may differ from the reference program's by a relative error of at most 0.0024.
Values may be sent and summed in bfloat16 or wider, within the bound.
A program may use at most 64 MiB of HBM per device.

```python
import math
import jax
import jax.numpy as jnp
from jax import lax

D = 768
MEM_DEV = 512
CLUSTERS = 4
DOC_DEV = 512
MEMBERS = 4096
N_CLUS = 4
N_WIDE = 8


def shuffled(sub_key):
    return jax.random.permutation(sub_key, MEM_DEV)


def member_layout(key):
    devices = N_CLUS * N_WIDE
    per_pair = MEM_DEV // devices
    half_count = devices // 2
    key_twist = jax.random.fold_in(key, 101)
    key_order = jax.random.fold_in(key, 102)
    key_rows = jax.random.fold_in(key, 103)
    key_members = jax.random.fold_in(key, 104)
    twist = jax.random.randint(key_twist, (half_count,), -per_pair, per_pair + 1)
    twist = twist.at[0].set(per_pair)
    profile = jnp.concatenate([per_pair + twist, per_pair - twist])
    profile = profile[jax.random.permutation(key_order, devices)]
    offsets = jnp.repeat(jnp.arange(devices, dtype=jnp.int32), profile, total_repeat_length=MEM_DEV)
    receivers = jnp.arange(devices, dtype=jnp.int32)[:, None]
    sources = (receivers + offsets[None, :]) % devices
    row_orders = jax.vmap(shuffled)(jax.random.split(key_rows, devices))
    picked = jnp.take_along_axis(row_orders[sources.reshape(-1)].reshape(devices, MEM_DEV, MEM_DEV), jnp.broadcast_to(jnp.arange(MEM_DEV, dtype=jnp.int32)[None, :, None], (devices, MEM_DEV, 1)), axis=2)[:, :, 0]
    member_orders = jax.vmap(shuffled)(jax.random.split(key_members, devices))
    sources = jnp.take_along_axis(sources, member_orders, axis=1)
    picked = jnp.take_along_axis(picked, member_orders, axis=1)
    return (sources.reshape(N_CLUS, MEM_DEV * N_WIDE).astype(jnp.int32), picked.reshape(N_CLUS, MEM_DEV * N_WIDE).astype(jnp.int32))


def draw_source_device(key, part):
    return member_layout(key)[0]


def draw_source_row(key, part):
    return member_layout(key)[1]


def draw_documents(key, part):
    sources, picked = member_layout(key)
    members = MEM_DEV * N_WIDE
    group_total = max(members // 4, 1)
    group_ids = jax.random.randint(jax.random.fold_in(key, 7), (N_CLUS, members), 0, group_total)
    group_ids = group_ids + jnp.arange(N_CLUS, dtype=jnp.int32)[:, None] * group_total
    prototypes = jax.random.normal(jax.random.fold_in(key, 8), (N_CLUS * group_total, D), jnp.float32)
    mixing = jax.random.uniform(jax.random.fold_in(key, 9), (N_CLUS, members, 1), jnp.float32, 0.0, 2.5)
    noise = jax.random.normal(jax.random.fold_in(key, 10), (N_CLUS, members, D), jnp.float32)
    scales = jnp.exp(jax.random.uniform(jax.random.fold_in(key, 12), (N_CLUS, members, 1), jnp.float32, 0.0, math.log(10.0)))
    vectors = (mixing * prototypes[group_ids] + noise) * scales
    target = (sources * MEM_DEV + picked).reshape(-1)
    flat = jnp.zeros((N_CLUS * N_WIDE * MEM_DEV, D), jnp.float32).at[target].set(vectors.reshape(-1, D))
    return jnp.clip(flat, -96.0, 96.0).astype(jnp.bfloat16)


def level_of(own_key, shape, cuts, least, top_value):
    factor_of, own = 1.0, jax.random.fold_in(own_key, 6)
    for dim, shards_of in cuts:
        draws = jnp.exp(jax.random.uniform(jax.random.fold_in(own, dim), (shards_of,), jnp.float32, least / len(cuts), top_value / len(cuts)))
        factor_of = factor_of * jnp.repeat(draws, shape[dim] // shards_of).reshape([-1 if axis == dim else 1 for axis in range(len(shape))])
    return factor_of


def normal_values(key, dims, scale, limit, cuts=(), held_as=jnp.bfloat16):
    factor_of = level_of(key, dims, cuts, -0.22, 0.18) if cuts else 1.0
    result = jax.random.normal(key, dims, jnp.float32) * scale * factor_of
    return jnp.minimum(jnp.maximum(result, -limit), limit).astype(held_as)


def setup_inputs(seed: int = 0) -> dict:
    key_of = jax.random.split(jax.random.key(seed), 5)
    return {
        "documents": draw_documents(jax.random.fold_in(key_of[4], 71), 0),
        "source_device": draw_source_device(jax.random.fold_in(key_of[4], 71), 0),
        "source_row": draw_source_row(jax.random.fold_in(key_of[4], 71), 0),
        "centroids": normal_values(key_of[3], (CLUSTERS, D), 1.0, 6.0, ((0, 4),), jnp.float32),
    }


def unit_rows(raw_rows):
    values = raw_rows.astype(jnp.float32)
    return values * lax.rsqrt(lax.optimization_barrier(jnp.sum(values * values, axis=-1, keepdims=True)) + 1e-06)

def nearest_in_cluster(stored):
    count = stored.shape[0]
    blocks = count // 512
    columns = jnp.arange(count, dtype=jnp.int32)

    def one_block(index):
        start = index * 512
        queries = lax.dynamic_slice_in_dim(stored, start, 512, 0)
        scores = jnp.dot(queries, stored.T, preferred_element_type=jnp.float32)
        rows_here = start + jnp.arange(512, dtype=jnp.int32)
        scores = jnp.where(columns[None, :] < rows_here[:, None], scores, -1.0)
        return lax.optimization_barrier(jnp.max(scores, axis=1))
    return lax.map(one_block, jnp.arange(blocks, dtype=jnp.int32)).reshape(count)

def reference(documents, source_device, source_row, centroids):
    position = (source_device * DOC_DEV + source_row).astype(jnp.int32)
    member_rows = jnp.take(documents, position.reshape(-1), axis=0).reshape(CLUSTERS, MEMBERS, D)
    unit = unit_rows(member_rows)
    direction = unit_rows(centroids)
    centroid_distance = 1.0 - lax.optimization_barrier(jnp.sum(unit * direction[:, None, :], axis=-1))
    stored = unit.astype(jnp.bfloat16)
    nearest_earlier = lax.map(nearest_in_cluster, stored)
    return (nearest_earlier, centroid_distance)
```

```python
import functools

import jax
import jax.numpy as jnp
from jax import lax
from jax.experimental import pallas as pl
from jax.experimental.pallas import tpu as pltpu
from jax.sharding import PartitionSpec as P

MESH = pl.DeviceIdType.MESH
LANES = 128


def iota(shape, dim):
    return lax.broadcasted_iota(jnp.int32, shape, dim)


def dot_nt(left, right):
    return lax.dot_general(
        left, right, (((1,), (1,)), ((), ())), preferred_element_type=jnp.float32
    )


def dot_nn(left, right):
    return jnp.dot(left, right, preferred_element_type=jnp.float32)


def as_column(row):
    return jnp.transpose(jnp.broadcast_to(row, (LANES, row.shape[1])))[:, :1]


def kernel(
    clusters, wide, cap, slots,
    docs_ref, sender_ref, row_ref, centroid_ref,
    near_ref, dist_ref,
    wanted, asked, place_out, place_in, cent_out, cent_in,
    outgoing, arrived, total, gathered, best, res_out, res_in,
    ask_send, ask_recv, info_send, info_recv, row_send, row_recv,
    block_send, block_recv, pass_send, res_send, res_recv,
):
    devices = clusters * wide
    members = sender_ref.shape[1]
    doc_rows, width = docs_ref.shape
    swapped = wide == 2 * clusters
    my_clus = lax.axis_index("clus")
    my_wide = lax.axis_index("wide")
    me = my_clus * wide + my_wide

    def role(device):
        if not swapped:
            return device
        first, rest = lax.div(device, wide), lax.rem(device, wide)
        return lax.div(rest, 2) * wide + 2 * first + lax.rem(rest, 2)

    def where_is(device):
        return (lax.div(device, wide), lax.rem(device, wide))

    def remote(src, dst, send, recv, device):
        return pltpu.make_async_remote_copy(
            src_ref=src, dst_ref=dst, send_sem=send, recv_sem=recv,
            device_id=where_is(device), device_id_type=MESH,
        )

    barrier = pltpu.get_barrier_semaphore()

    @pl.loop(1, devices)
    def _(t):
        other = lax.rem(me + t, devices)
        pl.semaphore_signal(barrier, inc=1, device_id=where_is(other), device_id_type=MESH)

    senders = sender_ref[...]
    same = iota((devices, members), 0) == senders
    one_hot = same.astype(jnp.float32)
    earlier = (iota((members, members), 0) < iota((members, members), 1)).astype(jnp.float32)
    rank = dot_nn(one_hot.astype(jnp.bfloat16), earlier.astype(jnp.bfloat16))
    slot = jnp.sum(jnp.where(same, rank, 0.0), axis=0, keepdims=True).astype(jnp.int32)
    place_out[...] = senders * slots + slot
    cent_out[...] = centroid_ref[...]
    at_slot = (iota((LANES, members), 0) == slot).astype(jnp.float32).astype(jnp.bfloat16)
    named = row_ref[...] + 1
    high = lax.shift_right_logical(named, 8)
    low = named - high * 256
    ask_low = dot_nt((one_hot * low.astype(jnp.float32)).astype(jnp.bfloat16), at_slot)
    ask_high = dot_nt((one_hot * high.astype(jnp.float32)).astype(jnp.bfloat16), at_slot)
    ask = (ask_low + 256.0 * ask_high).astype(jnp.int32)
    for s in range(devices):
        wanted[s] = ask[s:s + 1, :]

    pl.semaphore_wait(barrier, devices - 1)

    partner = role(me)
    asked[me] = wanted[me]

    @pl.loop(1, devices)
    def _(t):
        other = lax.rem(me + t, devices)
        remote(wanted.at[other], asked.at[me], ask_send.at[other], ask_recv.at[me], other).start()

    place_copy = remote(place_out, place_in, info_send.at[0], info_recv.at[0], partner)
    cent_copy = remote(cent_out, cent_in, info_send.at[1], info_recv.at[1], partner)

    @pl.when(partner != me)
    def _():
        place_copy.start()
        cent_copy.start()

    @pl.when(partner == me)
    def _():
        place_in[...] = place_out[...]
        cent_in[...] = cent_out[...]

    @pl.loop(1, devices)
    def _(t):
        other = lax.rem(me + devices - t, devices)
        remote(wanted.at[me], asked.at[other], ask_send.at[other], ask_recv.at[other], other).wait_recv()

    asked_t = jnp.transpose(asked[:, 0, :].astype(jnp.float32))
    doc_ids = (iota((slots, doc_rows), 1) + 1).astype(jnp.float32)
    docs = docs_ref[...]
    per_dot = max(1, LANES // slots)
    for first in range(0, devices, per_dot):
        chosen = jnp.concatenate(
            [
                (asked_t[:slots, o:o + 1] == doc_ids).astype(jnp.float32)
                for o in range(first, first + per_dot)
            ],
            axis=0,
        ).astype(jnp.bfloat16)
        rows = dot_nn(chosen, docs).astype(jnp.bfloat16)
        for i in range(per_dot):
            outgoing[first + i] = rows[i * slots:(i + 1) * slots]

    @pl.loop(1, devices)
    def _(t):
        holder = lax.rem(me + t, devices)
        remote(outgoing.at[role(holder)], arrived.at[me], row_send.at[holder], row_recv.at[me], holder).start()

    arrived[me] = outgoing[partner]

    @pl.when(partner != me)
    def _():
        place_copy.wait_recv()
        cent_copy.wait_recv()

    places = as_column(place_in[...].astype(jnp.float32))
    per_part = max(1, 256 // slots)
    for first in range(0, devices, per_part):
        for s in range(first, first + per_part):
            @pl.when(s != me)
            def _(s=s):
                remote(outgoing.at[s], arrived.at[s], row_send.at[s], row_recv.at[s], s).wait_recv()
        ids = (first * slots + iota((members, per_part * slots), 1)).astype(jnp.float32)
        pick = (places == ids).astype(jnp.float32).astype(jnp.bfloat16)
        part = dot_nn(pick, arrived[first:first + per_part].reshape(per_part * slots, width))
        if first == 0:
            total[...] = part
        else:
            total[...] += part

    block = lax.rem(partner, wide)
    cluster = lax.div(partner, wide)
    values = total[...]
    unit = values * lax.rsqrt(jnp.sum(values * values, axis=1, keepdims=True) + 1e-06)
    centroid = cent_in[...]
    direction = centroid * lax.rsqrt(jnp.sum(centroid * centroid, axis=1, keepdims=True) + 1e-06)
    distance = 1.0 - jnp.sum(unit * direction, axis=1, keepdims=True)
    gathered[block] = unit.astype(jnp.bfloat16)

    chips = wide // 2
    chip, core = lax.div(block, 2), lax.rem(block, 2)
    sibling = role(cluster * wide + 2 * chip + 1 - core)

    def holder_of(some_chip):
        return role(cluster * wide + 2 * some_chip + core)

    def block_copy(target_chip):
        return remote(gathered.at[block], gathered.at[block], block_send.at[target_chip],
                      block_recv.at[block], holder_of(target_chip))

    def sibling_copy(which):
        return remote(gathered.at[which], gathered.at[which], pass_send.at[which],
                      block_recv.at[which], sibling)

    @pl.loop(chip + 1, chips)
    def _(later):
        block_copy(later).start()

    @pl.when(core == 0)
    def _():
        sibling_copy(block).start()

    def fold(scores):
        out = scores[:, :LANES]
        for i in range(1, members // LANES):
            out = jnp.maximum(out, scores[:, i * LANES:(i + 1) * LANES])
        return out

    mine = gathered[block]
    scores = dot_nt(mine, mine)
    scores = jnp.where(iota((members, members), 1) < iota((members, members), 0), scores, -1.0)
    best[...] = jnp.maximum(fold(scores), -1.0)

    def meet(which):
        best[...] = jnp.maximum(best[...], fold(dot_nt(gathered[block], gathered[which])))

    @pl.when(core == 1)
    def _():
        sibling_copy(2 * chip).wait_recv()
        meet(2 * chip)

    @pl.loop(0, chip)
    def _(t):
        direct = 2 * (chip - 1 - t) + core
        sibling_copy(direct).wait_recv()
        sibling_copy(direct).start()
        meet(direct)
        passed = 2 * (chip - 1 - t) + 1 - core
        sibling_copy(passed).wait_recv()
        meet(passed)

    nearest = jnp.max(best[...], axis=1, keepdims=True)
    column = iota((members, LANES), 1)
    both = jnp.transpose(jnp.where(column == 0, nearest, distance))
    res_out[...] = both[:8]

    res_copy = remote(res_out, res_in, res_send, res_recv, partner)

    @pl.when(partner != me)
    def _():
        res_copy.start()
        res_copy.wait_recv()

    @pl.when(partner == me)
    def _():
        res_in[...] = res_out[...]

    near_ref[...] = res_in[0:1, :]
    dist_ref[...] = res_in[1:2, :]

    @pl.when(partner != me)
    def _():
        res_copy.wait_send()
        place_copy.wait_send()
        cent_copy.wait_send()

    @pl.loop(1, devices)
    def _(t):
        other = lax.rem(me + t, devices)
        remote(wanted.at[other], asked.at[me], ask_send.at[other], ask_recv.at[me], other).wait_send()
        remote(outgoing.at[other], arrived.at[me], row_send.at[other], row_recv.at[me], other).wait_send()

    @pl.loop(chip + 1, chips)
    def _(later):
        block_copy(later).wait_send()

    @pl.when(core == 0)
    def _():
        sibling_copy(block).wait_send()

    @pl.loop(0, chip)
    def _(t):
        sibling_copy(2 * (chip - 1 - t) + core).wait_send()


def solution(mesh):
    clusters, wide = mesh.shape["clus"], mesh.shape["wide"]
    devices = clusters * wide

    def on_device(documents, source_device, source_row, centroids):
        members = source_device.shape[1]
        width = documents.shape[1]
        cap = 2 * members // devices
        slots = max(16, cap)
        dma = pltpu.SemaphoreType.DMA
        f32, bf16, i32 = jnp.float32, jnp.bfloat16, jnp.int32
        vmem = pl.BlockSpec(memory_space=pltpu.VMEM)
        return pl.pallas_call(
            functools.partial(kernel, clusters, wide, cap, slots),
            out_shape=[jax.ShapeDtypeStruct((1, members), f32)] * 2,
            in_specs=[vmem] * 4,
            out_specs=[vmem] * 2,
            scratch_shapes=[
                pltpu.VMEM((devices, 1, LANES), i32),
                pltpu.VMEM((devices, 1, LANES), i32),
                pltpu.VMEM((1, members), i32),
                pltpu.VMEM((1, members), i32),
                pltpu.VMEM((1, width), f32),
                pltpu.VMEM((1, width), f32),
                pltpu.VMEM((devices, slots, width), bf16),
                pltpu.VMEM((devices, slots, width), bf16),
                pltpu.VMEM((members, width), f32),
                pltpu.VMEM((wide, members, width), bf16),
                pltpu.VMEM((members, LANES), f32),
                pltpu.VMEM((8, members), f32),
                pltpu.VMEM((8, members), f32),
                dma((devices,)), dma((devices,)), dma((2,)), dma((2,)),
                dma((devices,)), dma((devices,)),
                dma((wide // 2,)), dma((wide,)), dma((wide,)), dma, dma,
            ],
            compiler_params=pltpu.CompilerParams(
                collective_id=0, has_side_effects=True, vmem_limit_bytes=56 * 1024 * 1024
            ),
        )(documents, source_device, source_row, centroids)

    placed = (P(("clus", "wide"), None), P("clus", "wide"), P("clus", "wide"), P("clus", None))
    return jax.shard_map(
        on_device,
        mesh=mesh,
        in_specs=placed,
        out_specs=(P("clus", "wide"), P("clus", "wide")),
        check_vma=False,
    )
```

```python
import functools

import jax
import jax.numpy as jnp
from jax import lax
from jax.experimental import pallas as pl
from jax.experimental.pallas import tpu as pltpu
from jax.sharding import PartitionSpec as P

MESH = pl.DeviceIdType.MESH
LANES = 128


def iota(shape, dim):
    return lax.broadcasted_iota(jnp.int32, shape, dim)


def dot_nt(left, right):
    return lax.dot_general(
        left, right, (((1,), (1,)), ((), ())), preferred_element_type=jnp.float32
    )


def dot_nn(left, right):
    return jnp.dot(left, right, preferred_element_type=jnp.float32)


def as_column(row):
    return jnp.transpose(jnp.broadcast_to(row, (LANES, row.shape[1])))[:, :1]


def kernel(
    clusters, wide, cap, slots,
    docs_ref, sender_ref, row_ref, centroid_ref,
    near_ref, dist_ref,
    wanted, asked, place_out, place_in, cent_out, cent_in,
    outgoing, arrived, total, gathered, best, res_out, res_in,
    ask_send, ask_recv, info_send, info_recv, row_send, row_recv,
    block_send, block_recv, pass_send, relay_send, res_send, res_recv,
):
    devices = clusters * wide
    members = sender_ref.shape[1]
    doc_rows, width = docs_ref.shape
    swapped = wide == 2 * clusters
    my_clus = lax.axis_index("clus")
    my_wide = lax.axis_index("wide")
    me = my_clus * wide + my_wide

    def role(device):
        if not swapped:
            return device
        first, rest = lax.div(device, wide), lax.rem(device, wide)
        return lax.div(rest, 2) * wide + 2 * first + lax.rem(rest, 2)

    def where_is(device):
        return (lax.div(device, wide), lax.rem(device, wide))

    def remote(src, dst, send, recv, device):
        return pltpu.make_async_remote_copy(
            src_ref=src, dst_ref=dst, send_sem=send, recv_sem=recv,
            device_id=where_is(device), device_id_type=MESH,
        )

    barrier = pltpu.get_barrier_semaphore()

    @pl.loop(1, devices)
    def _(t):
        other = lax.rem(me + t, devices)
        pl.semaphore_signal(barrier, inc=1, device_id=where_is(other), device_id_type=MESH)

    senders = sender_ref[...]
    same = iota((devices, members), 0) == senders
    one_hot = same.astype(jnp.float32)
    earlier = (iota((members, members), 0) < iota((members, members), 1)).astype(jnp.float32)
    rank = dot_nn(one_hot.astype(jnp.bfloat16), earlier.astype(jnp.bfloat16))
    slot = jnp.sum(jnp.where(same, rank, 0.0), axis=0, keepdims=True).astype(jnp.int32)
    place_out[...] = senders * slots + slot
    cent_out[...] = centroid_ref[...]
    at_slot = (iota((LANES, members), 0) == slot).astype(jnp.float32).astype(jnp.bfloat16)
    named = row_ref[...] + 1
    high = lax.shift_right_logical(named, 8)
    low = named - high * 256
    ask_low = dot_nt((one_hot * low.astype(jnp.float32)).astype(jnp.bfloat16), at_slot)
    ask_high = dot_nt((one_hot * high.astype(jnp.float32)).astype(jnp.bfloat16), at_slot)
    ask = (ask_low + 256.0 * ask_high).astype(jnp.int32)
    for s in range(devices):
        wanted[s] = ask[s:s + 1, :]

    pl.semaphore_wait(barrier, devices - 1)

    partner = role(me)
    asked[me] = wanted[me]

    @pl.loop(1, devices)
    def _(t):
        other = lax.rem(me + t, devices)
        remote(wanted.at[other], asked.at[me], ask_send.at[other], ask_recv.at[me], other).start()

    place_copy = remote(place_out, place_in, info_send.at[0], info_recv.at[0], partner)
    cent_copy = remote(cent_out, cent_in, info_send.at[1], info_recv.at[1], partner)

    @pl.when(partner != me)
    def _():
        place_copy.start()
        cent_copy.start()

    @pl.when(partner == me)
    def _():
        place_in[...] = place_out[...]
        cent_in[...] = cent_out[...]

    @pl.loop(1, devices)
    def _(t):
        other = lax.rem(me + devices - t, devices)
        remote(wanted.at[me], asked.at[other], ask_send.at[other], ask_recv.at[other], other).wait_recv()

    asked_t = jnp.transpose(asked[:, 0, :].astype(jnp.float32))
    doc_ids = (iota((slots, doc_rows), 1) + 1).astype(jnp.float32)
    docs = docs_ref[...]
    per_dot = max(1, LANES // slots)
    for first in range(0, devices, per_dot):
        chosen = jnp.concatenate(
            [
                (asked_t[:slots, o:o + 1] == doc_ids).astype(jnp.float32)
                for o in range(first, first + per_dot)
            ],
            axis=0,
        ).astype(jnp.bfloat16)
        rows = dot_nn(chosen, docs).astype(jnp.bfloat16)
        for i in range(per_dot):
            outgoing[first + i] = rows[i * slots:(i + 1) * slots]

    @pl.loop(1, devices)
    def _(t):
        holder = lax.rem(me + t, devices)
        remote(outgoing.at[role(holder)], arrived.at[me], row_send.at[holder], row_recv.at[me], holder).start()

    arrived[me] = outgoing[partner]

    @pl.when(partner != me)
    def _():
        place_copy.wait_recv()
        cent_copy.wait_recv()

    places = as_column(place_in[...].astype(jnp.float32))
    per_part = max(1, 256 // slots)
    for first in range(0, devices, per_part):
        for s in range(first, first + per_part):
            @pl.when(s != me)
            def _(s=s):
                remote(outgoing.at[s], arrived.at[s], row_send.at[s], row_recv.at[s], s).wait_recv()
        ids = (first * slots + iota((members, per_part * slots), 1)).astype(jnp.float32)
        pick = (places == ids).astype(jnp.float32).astype(jnp.bfloat16)
        part = dot_nn(pick, arrived[first:first + per_part].reshape(per_part * slots, width))
        if first == 0:
            total[...] = part
        else:
            total[...] += part

    block = lax.rem(partner, wide)
    cluster = lax.div(partner, wide)
    values = total[...]
    unit = values * lax.rsqrt(jnp.sum(values * values, axis=1, keepdims=True) + 1e-06)
    centroid = cent_in[...]
    direction = centroid * lax.rsqrt(jnp.sum(centroid * centroid, axis=1, keepdims=True) + 1e-06)
    distance = 1.0 - jnp.sum(unit * direction, axis=1, keepdims=True)
    gathered[block] = unit.astype(jnp.bfloat16)

    chips = wide // 2
    chip, core = lax.div(block, 2), lax.rem(block, 2)
    sibling = role(cluster * wide + 2 * chip + 1 - core)

    def holder_of(some_chip):
        return role(cluster * wide + 2 * some_chip + core)

    def block_copy(target_chip):
        return remote(gathered.at[block], gathered.at[block], block_send.at[target_chip],
                      block_recv.at[block], holder_of(target_chip))

    def sibling_copy(which):
        return remote(gathered.at[which], gathered.at[which], pass_send.at[which],
                      block_recv.at[which], sibling)

    relayed = swapped and chips == 4

    def goes_direct(later):
        if not relayed:
            return later >= 0
        by_third = ((chip == 0) & (later == 3)) | ((chip == 1) & (later == 2) & (core == 1))
        return jnp.logical_not(by_third)

    relay_block = jnp.where(chip == 1, 0, jnp.where(chip == 2, 1, 3))
    relays = ((chip == 1) & (core == 0)) | ((chip >= 2) & (core == 1))
    relay_copy = remote(gathered.at[relay_block], gathered.at[relay_block], relay_send,
                        block_recv.at[relay_block], holder_of(jnp.where(chip == 3, 2, 3)))

    def source_chip(t):
        if not relayed:
            return chip - 1 - t
        return jnp.where(chip == 2, t, chip - 1 - t)

    @pl.loop(chip + 1, chips)
    def _(later):
        @pl.when(goes_direct(later))
        def _():
            block_copy(later).start()

    @pl.when(core == 0)
    def _():
        sibling_copy(block).start()

    def fold(scores):
        out = scores[:, :LANES]
        for i in range(1, members // LANES):
            out = jnp.maximum(out, scores[:, i * LANES:(i + 1) * LANES])
        return out

    mine = gathered[block]
    scores = dot_nt(mine, mine)
    scores = jnp.where(iota((members, members), 1) < iota((members, members), 0), scores, -1.0)
    best[...] = jnp.maximum(fold(scores), -1.0)

    def meet(which):
        best[...] = jnp.maximum(best[...], fold(dot_nt(gathered[block], gathered[which])))

    @pl.when(core == 1)
    def _():
        sibling_copy(2 * chip).wait_recv()
        meet(2 * chip)

    @pl.loop(0, chip)
    def _(t):
        direct = 2 * source_chip(t) + core
        sibling_copy(direct).wait_recv()
        if relayed:
            @pl.when(relays & (direct == relay_block))
            def _():
                relay_copy.start()
        sibling_copy(direct).start()
        meet(direct)
        passed = 2 * source_chip(t) + 1 - core
        sibling_copy(passed).wait_recv()
        meet(passed)

    nearest = jnp.max(best[...], axis=1, keepdims=True)
    column = iota((members, LANES), 1)
    both = jnp.transpose(jnp.where(column == 0, nearest, distance))
    res_out[...] = both[:8]

    res_copy = remote(res_out, res_in, res_send, res_recv, partner)

    @pl.when(partner != me)
    def _():
        res_copy.start()
        res_copy.wait_recv()

    @pl.when(partner == me)
    def _():
        res_in[...] = res_out[...]

    near_ref[...] = res_in[0:1, :]
    dist_ref[...] = res_in[1:2, :]

    @pl.when(partner != me)
    def _():
        res_copy.wait_send()
        place_copy.wait_send()
        cent_copy.wait_send()

    @pl.loop(1, devices)
    def _(t):
        other = lax.rem(me + t, devices)
        remote(wanted.at[other], asked.at[me], ask_send.at[other], ask_recv.at[me], other).wait_send()
        remote(outgoing.at[other], arrived.at[me], row_send.at[other], row_recv.at[me], other).wait_send()

    @pl.loop(chip + 1, chips)
    def _(later):
        @pl.when(goes_direct(later))
        def _():
            block_copy(later).wait_send()

    if relayed:
        @pl.when(relays)
        def _():
            relay_copy.wait_send()

    @pl.when(core == 0)
    def _():
        sibling_copy(block).wait_send()

    @pl.loop(0, chip)
    def _(t):
        sibling_copy(2 * (chip - 1 - t) + core).wait_send()


def solution(mesh):
    clusters, wide = mesh.shape["clus"], mesh.shape["wide"]
    devices = clusters * wide

    def on_device(documents, source_device, source_row, centroids):
        members = source_device.shape[1]
        width = documents.shape[1]
        cap = 2 * members // devices
        slots = max(16, cap)
        dma = pltpu.SemaphoreType.DMA
        f32, bf16, i32 = jnp.float32, jnp.bfloat16, jnp.int32
        vmem = pl.BlockSpec(memory_space=pltpu.VMEM)
        return pl.pallas_call(
            functools.partial(kernel, clusters, wide, cap, slots),
            out_shape=[jax.ShapeDtypeStruct((1, members), f32)] * 2,
            in_specs=[vmem] * 4,
            out_specs=[vmem] * 2,
            scratch_shapes=[
                pltpu.VMEM((devices, 1, LANES), i32),
                pltpu.VMEM((devices, 1, LANES), i32),
                pltpu.VMEM((1, members), i32),
                pltpu.VMEM((1, members), i32),
                pltpu.VMEM((1, width), f32),
                pltpu.VMEM((1, width), f32),
                pltpu.VMEM((devices, slots, width), bf16),
                pltpu.VMEM((devices, slots, width), bf16),
                pltpu.VMEM((members, width), f32),
                pltpu.VMEM((wide, members, width), bf16),
                pltpu.VMEM((members, LANES), f32),
                pltpu.VMEM((8, members), f32),
                pltpu.VMEM((8, members), f32),
                dma((devices,)), dma((devices,)), dma((2,)), dma((2,)),
                dma((devices,)), dma((devices,)),
                dma((wide // 2,)), dma((wide,)), dma((wide,)), dma, dma, dma,
            ],
            compiler_params=pltpu.CompilerParams(
                collective_id=0, has_side_effects=True, vmem_limit_bytes=56 * 1024 * 1024
            ),
        )(documents, source_device, source_row, centroids)

    placed = (P(("clus", "wide"), None), P("clus", "wide"), P("clus", "wide"), P("clus", None))
    return jax.shard_map(
        on_device,
        mesh=mesh,
        in_specs=placed,
        out_specs=(P("clus", "wide"), P("clus", "wide")),
        check_vma=False,
    )
```

```python
import functools

import jax
import jax.numpy as jnp
from jax import lax
from jax.experimental import pallas as pl
from jax.experimental.pallas import tpu as pltpu
from jax.sharding import PartitionSpec as P

MESH = pl.DeviceIdType.MESH
LANES = 128


def iota(shape, dim):
    return lax.broadcasted_iota(jnp.int32, shape, dim)


def dot_nt(left, right):
    return lax.dot_general(
        left, right, (((1,), (1,)), ((), ())), preferred_element_type=jnp.float32
    )


def dot_nn(left, right):
    return jnp.dot(left, right, preferred_element_type=jnp.float32)


def as_column(row):
    return jnp.transpose(jnp.broadcast_to(row, (LANES, row.shape[1])))[:, :1]


def kernel(
    clusters, wide, cap, slots,
    docs_ref, sender_ref, row_ref, centroid_ref,
    near_ref, dist_ref,
    wanted, asked, place_out, place_in, cent_out, cent_in,
    outgoing, arrived, total, gathered, best, res_out, res_in,
    ask_send, ask_recv, info_send, info_recv, row_send, row_recv,
    block_send, block_recv, pass_send, res_send, res_recv,
):
    devices = clusters * wide
    members = sender_ref.shape[1]
    doc_rows, width = docs_ref.shape
    swapped = wide == 2 * clusters
    my_clus = lax.axis_index("clus")
    my_wide = lax.axis_index("wide")
    me = my_clus * wide + my_wide

    def role(device):
        if not swapped:
            return device
        first, rest = lax.div(device, wide), lax.rem(device, wide)
        return lax.div(rest, 2) * wide + 2 * first + lax.rem(rest, 2)

    def where_is(device):
        return (lax.div(device, wide), lax.rem(device, wide))

    def remote(src, dst, send, recv, device):
        return pltpu.make_async_remote_copy(
            src_ref=src, dst_ref=dst, send_sem=send, recv_sem=recv,
            device_id=where_is(device), device_id_type=MESH,
        )

    barrier = pltpu.get_barrier_semaphore()

    @pl.loop(1, devices)
    def _(t):
        other = lax.rem(me + t, devices)
        pl.semaphore_signal(barrier, inc=1, device_id=where_is(other), device_id_type=MESH)

    senders = sender_ref[...]
    same = iota((devices, members), 0) == senders
    one_hot = same.astype(jnp.float32)
    earlier = (iota((members, members), 0) < iota((members, members), 1)).astype(jnp.float32)
    rank = dot_nn(one_hot.astype(jnp.bfloat16), earlier.astype(jnp.bfloat16))
    slot = jnp.sum(jnp.where(same, rank, 0.0), axis=0, keepdims=True).astype(jnp.int32)
    place_out[...] = senders * slots + slot
    cent_out[...] = centroid_ref[...]
    at_slot = (iota((LANES, members), 0) == slot).astype(jnp.float32).astype(jnp.bfloat16)
    named = row_ref[...] + 1
    high = lax.shift_right_logical(named, 8)
    low = named - high * 256
    ask_low = dot_nt((one_hot * low.astype(jnp.float32)).astype(jnp.bfloat16), at_slot)
    ask_high = dot_nt((one_hot * high.astype(jnp.float32)).astype(jnp.bfloat16), at_slot)
    ask = (ask_low + 256.0 * ask_high).astype(jnp.int32)
    for s in range(devices):
        wanted[s] = ask[s:s + 1, :]

    pl.semaphore_wait(barrier, devices - 1)

    partner = role(me)
    asked[me] = wanted[me]

    @pl.loop(1, devices)
    def _(t):
        other = lax.rem(me + t, devices)
        remote(wanted.at[other], asked.at[me], ask_send.at[other], ask_recv.at[me], other).start()

    place_copy = remote(place_out, place_in, info_send.at[0], info_recv.at[0], partner)
    cent_copy = remote(cent_out, cent_in, info_send.at[1], info_recv.at[1], partner)

    @pl.when(partner != me)
    def _():
        place_copy.start()
        cent_copy.start()

    @pl.when(partner == me)
    def _():
        place_in[...] = place_out[...]
        cent_in[...] = cent_out[...]

    @pl.loop(1, devices)
    def _(t):
        other = lax.rem(me + devices - t, devices)
        remote(wanted.at[me], asked.at[other], ask_send.at[other], ask_recv.at[other], other).wait_recv()

    asked_t = jnp.transpose(asked[:, 0, :].astype(jnp.float32))
    doc_ids = (iota((slots, doc_rows), 1) + 1).astype(jnp.float32)
    docs = docs_ref[...]
    per_dot = max(1, LANES // slots)
    for first in range(0, devices, per_dot):
        chosen = jnp.concatenate(
            [
                (asked_t[:slots, o:o + 1] == doc_ids).astype(jnp.float32)
                for o in range(first, first + per_dot)
            ],
            axis=0,
        ).astype(jnp.bfloat16)
        rows = dot_nn(chosen, docs).astype(jnp.bfloat16)
        for i in range(per_dot):
            outgoing[first + i] = rows[i * slots:(i + 1) * slots]

    @pl.loop(1, devices)
    def _(t):
        holder = lax.rem(me + t, devices)
        remote(outgoing.at[role(holder)], arrived.at[me], row_send.at[holder], row_recv.at[me], holder).start()

    arrived[me] = outgoing[partner]

    @pl.when(partner != me)
    def _():
        place_copy.wait_recv()
        cent_copy.wait_recv()

    places = as_column(place_in[...].astype(jnp.float32))
    per_part = max(1, 256 // slots)
    for first in range(0, devices, per_part):
        for s in range(first, first + per_part):
            @pl.when(s != me)
            def _(s=s):
                remote(outgoing.at[s], arrived.at[s], row_send.at[s], row_recv.at[s], s).wait_recv()
        ids = (first * slots + iota((members, per_part * slots), 1)).astype(jnp.float32)
        pick = (places == ids).astype(jnp.float32).astype(jnp.bfloat16)
        part = dot_nn(pick, arrived[first:first + per_part].reshape(per_part * slots, width))
        if first == 0:
            total[...] = part
        else:
            total[...] += part

    block = lax.rem(partner, wide)
    cluster = lax.div(partner, wide)
    values = total[...]
    unit = values * lax.rsqrt(jnp.sum(values * values, axis=1, keepdims=True) + 1e-06)
    centroid = cent_in[...]
    direction = centroid * lax.rsqrt(jnp.sum(centroid * centroid, axis=1, keepdims=True) + 1e-06)
    distance = 1.0 - jnp.sum(unit * direction, axis=1, keepdims=True)
    mine = unit.astype(jnp.bfloat16)
    half = members // 2
    gathered[2 * block] = mine[:half]
    gathered[2 * block + 1] = mine[half:]

    chips = wide // 2
    chip, core = lax.div(block, 2), lax.rem(block, 2)
    sibling = role(cluster * wide + 2 * chip + 1 - core)

    def holder_of(some_chip):
        return role(cluster * wide + 2 * some_chip + core)

    def block_copy(target_chip, h):
        part = 2 * block + h
        return remote(gathered.at[part], gathered.at[part], block_send.at[2 * target_chip + h],
                      block_recv.at[part], holder_of(target_chip))

    def sibling_copy(which):
        return remote(gathered.at[which], gathered.at[which], pass_send.at[which],
                      block_recv.at[which], sibling)

    @pl.loop(chip + 1, chips)
    def _(later):
        block_copy(later, 0).start()

    @pl.loop(chip + 1, chips)
    def _(later):
        block_copy(later, 1).start()

    @pl.when(core == 0)
    def _():
        sibling_copy(2 * block).start()
        sibling_copy(2 * block + 1).start()

    def fold(scores):
        out = scores[:, :LANES]
        for i in range(1, scores.shape[1] // LANES):
            out = jnp.maximum(out, scores[:, i * LANES:(i + 1) * LANES])
        return out

    scores = dot_nt(mine, mine)
    scores = jnp.where(iota((members, members), 1) < iota((members, members), 0), scores, -1.0)
    best[...] = jnp.maximum(fold(scores), -1.0)

    def meet(which):
        best[...] = jnp.maximum(best[...], fold(dot_nt(gathered[pl.ds(2 * block, 2)].reshape(members, width), gathered[which])))

    @pl.when(core == 1)
    def _():
        for h in range(2):
            sibling_copy(4 * chip + h).wait_recv()
            meet(4 * chip + h)

    for h in range(2):
        @pl.loop(0, chip)
        def _(t, h=h):
            direct = 2 * (2 * (chip - 1 - t) + core) + h
            sibling_copy(direct).wait_recv()
            sibling_copy(direct).start()
            meet(direct)
            passed = 2 * (2 * (chip - 1 - t) + 1 - core) + h
            sibling_copy(passed).wait_recv()
            meet(passed)

    nearest = jnp.max(best[...], axis=1, keepdims=True)
    column = iota((members, LANES), 1)
    both = jnp.transpose(jnp.where(column == 0, nearest, distance))
    res_out[...] = both[:8]

    res_copy = remote(res_out, res_in, res_send, res_recv, partner)

    @pl.when(partner != me)
    def _():
        res_copy.start()
        res_copy.wait_recv()

    @pl.when(partner == me)
    def _():
        res_in[...] = res_out[...]

    near_ref[...] = res_in[0:1, :]
    dist_ref[...] = res_in[1:2, :]

    @pl.when(partner != me)
    def _():
        res_copy.wait_send()
        place_copy.wait_send()
        cent_copy.wait_send()

    @pl.loop(1, devices)
    def _(t):
        other = lax.rem(me + t, devices)
        remote(wanted.at[other], asked.at[me], ask_send.at[other], ask_recv.at[me], other).wait_send()
        remote(outgoing.at[other], arrived.at[me], row_send.at[other], row_recv.at[me], other).wait_send()

    @pl.loop(chip + 1, chips)
    def _(later):
        block_copy(later, 0).wait_send()
        block_copy(later, 1).wait_send()

    @pl.when(core == 0)
    def _():
        sibling_copy(2 * block).wait_send()
        sibling_copy(2 * block + 1).wait_send()

    @pl.loop(0, chip)
    def _(t):
        for h in range(2):
            sibling_copy(2 * (2 * (chip - 1 - t) + core) + h).wait_send()


def solution(mesh):
    clusters, wide = mesh.shape["clus"], mesh.shape["wide"]
    devices = clusters * wide

    def on_device(documents, source_device, source_row, centroids):
        members = source_device.shape[1]
        width = documents.shape[1]
        cap = 2 * members // devices
        slots = max(16, cap)
        dma = pltpu.SemaphoreType.DMA
        f32, bf16, i32 = jnp.float32, jnp.bfloat16, jnp.int32
        vmem = pl.BlockSpec(memory_space=pltpu.VMEM)
        return pl.pallas_call(
            functools.partial(kernel, clusters, wide, cap, slots),
            out_shape=[jax.ShapeDtypeStruct((1, members), f32)] * 2,
            in_specs=[vmem] * 4,
            out_specs=[vmem] * 2,
            scratch_shapes=[
                pltpu.VMEM((devices, 1, LANES), i32),
                pltpu.VMEM((devices, 1, LANES), i32),
                pltpu.VMEM((1, members), i32),
                pltpu.VMEM((1, members), i32),
                pltpu.VMEM((1, width), f32),
                pltpu.VMEM((1, width), f32),
                pltpu.VMEM((devices, slots, width), bf16),
                pltpu.VMEM((devices, slots, width), bf16),
                pltpu.VMEM((members, width), f32),
                pltpu.VMEM((2 * wide, members // 2, width), bf16),
                pltpu.VMEM((members, LANES), f32),
                pltpu.VMEM((8, members), f32),
                pltpu.VMEM((8, members), f32),
                dma((devices,)), dma((devices,)), dma((2,)), dma((2,)),
                dma((devices,)), dma((devices,)),
                dma((wide,)), dma((2 * wide,)), dma((2 * wide,)), dma, dma,
            ],
            compiler_params=pltpu.CompilerParams(
                collective_id=0, has_side_effects=True, vmem_limit_bytes=56 * 1024 * 1024
            ),
        )(documents, source_device, source_row, centroids)

    placed = (P(("clus", "wide"), None), P("clus", "wide"), P("clus", "wide"), P("clus", None))
    return jax.shard_map(
        on_device,
        mesh=mesh,
        in_specs=placed,
        out_specs=(P("clus", "wide"), P("clus", "wide")),
        check_vma=False,
    )
```

```python
import functools

import jax
import jax.numpy as jnp
from jax import lax
from jax.experimental import pallas as pl
from jax.experimental.pallas import tpu as pltpu
from jax.sharding import PartitionSpec as P

MESH = pl.DeviceIdType.MESH
LANES = 128


def iota(shape, dim):
    return lax.broadcasted_iota(jnp.int32, shape, dim)


def dot_nt(left, right):
    return lax.dot_general(
        left, right, (((1,), (1,)), ((), ())), preferred_element_type=jnp.float32
    )


def dot_nn(left, right):
    return jnp.dot(left, right, preferred_element_type=jnp.float32)


def as_column(row):
    return jnp.transpose(jnp.broadcast_to(row, (LANES, row.shape[1])))[:, :1]


def kernel(
    clusters, wide, cap, slots,
    docs_ref, sender_ref, row_ref, centroid_ref,
    near_ref, dist_ref,
    wanted, asked, place_out, place_in, cent_out, cent_in,
    outgoing, arrived, total, gathered, own, scales, best, res_out, res_in,
    ask_send, ask_recv, info_send, info_recv, row_send, row_recv,
    block_send, block_recv, pass_send, scale_send, scale_recv, res_send, res_recv,
):
    devices = clusters * wide
    members = sender_ref.shape[1]
    doc_rows, width = docs_ref.shape
    part = width // 2
    swapped = wide == 2 * clusters
    my_clus = lax.axis_index("clus")
    my_wide = lax.axis_index("wide")
    me = my_clus * wide + my_wide

    def role(device):
        if not swapped:
            return device
        first, rest = lax.div(device, wide), lax.rem(device, wide)
        return lax.div(rest, 2) * wide + 2 * first + lax.rem(rest, 2)

    def where_is(device):
        return (lax.div(device, wide), lax.rem(device, wide))

    def remote(src, dst, send, recv, device):
        return pltpu.make_async_remote_copy(
            src_ref=src, dst_ref=dst, send_sem=send, recv_sem=recv,
            device_id=where_is(device), device_id_type=MESH,
        )

    barrier = pltpu.get_barrier_semaphore()

    @pl.loop(1, devices)
    def _(t):
        other = lax.rem(me + t, devices)
        pl.semaphore_signal(barrier, inc=1, device_id=where_is(other), device_id_type=MESH)

    senders = sender_ref[...]
    same = iota((devices, members), 0) == senders
    one_hot = same.astype(jnp.float32)
    earlier = (iota((members, members), 0) < iota((members, members), 1)).astype(jnp.float32)
    rank = dot_nn(one_hot.astype(jnp.bfloat16), earlier.astype(jnp.bfloat16))
    slot = jnp.sum(jnp.where(same, rank, 0.0), axis=0, keepdims=True).astype(jnp.int32)
    place_out[...] = senders * slots + slot
    cent_out[...] = centroid_ref[...]
    at_slot = (iota((LANES, members), 0) == slot).astype(jnp.float32).astype(jnp.bfloat16)
    named = row_ref[...] + 1
    high = lax.shift_right_logical(named, 8)
    low = named - high * 256
    ask_low = dot_nt((one_hot * low.astype(jnp.float32)).astype(jnp.bfloat16), at_slot)
    ask_high = dot_nt((one_hot * high.astype(jnp.float32)).astype(jnp.bfloat16), at_slot)
    ask = (ask_low + 256.0 * ask_high).astype(jnp.int32)
    for s in range(devices):
        wanted[s] = ask[s:s + 1, :]

    pl.semaphore_wait(barrier, devices - 1)

    partner = role(me)
    asked[me] = wanted[me]

    @pl.loop(1, devices)
    def _(t):
        other = lax.rem(me + t, devices)
        remote(wanted.at[other], asked.at[me], ask_send.at[other], ask_recv.at[me], other).start()

    place_copy = remote(place_out, place_in, info_send.at[0], info_recv.at[0], partner)
    cent_copy = remote(cent_out, cent_in, info_send.at[1], info_recv.at[1], partner)

    @pl.when(partner != me)
    def _():
        place_copy.start()
        cent_copy.start()

    @pl.when(partner == me)
    def _():
        place_in[...] = place_out[...]
        cent_in[...] = cent_out[...]

    @pl.loop(1, devices)
    def _(t):
        other = lax.rem(me + devices - t, devices)
        remote(wanted.at[me], asked.at[other], ask_send.at[other], ask_recv.at[other], other).wait_recv()

    asked_t = jnp.transpose(asked[:, 0, :].astype(jnp.float32))
    doc_ids = (iota((slots, doc_rows), 1) + 1).astype(jnp.float32)
    docs = docs_ref[...]
    per_dot = max(1, LANES // slots)
    for first in range(0, devices, per_dot):
        chosen = jnp.concatenate(
            [
                (asked_t[:slots, o:o + 1] == doc_ids).astype(jnp.float32)
                for o in range(first, first + per_dot)
            ],
            axis=0,
        ).astype(jnp.bfloat16)
        rows = dot_nn(chosen, docs).astype(jnp.bfloat16)
        for i in range(per_dot):
            outgoing[first + i] = rows[i * slots:(i + 1) * slots, :part]
            outgoing[devices + first + i] = rows[i * slots:(i + 1) * slots, part:]

    def row_copy(holder, h):
        return remote(outgoing.at[h * devices + role(holder)], arrived.at[h * devices + me],
                      row_send.at[h * devices + holder], row_recv.at[h * devices + me], holder)

    def row_arrival(source, h):
        at = h * devices + source
        return remote(outgoing.at[at], arrived.at[at], row_send.at[at], row_recv.at[at], source)

    @pl.loop(1, devices)
    def _(t):
        row_copy(lax.rem(me + t, devices), 0).start()

    arrived[me] = outgoing[partner]
    arrived[devices + me] = outgoing[devices + partner]

    @pl.loop(1, devices)
    def _(t):
        row_copy(lax.rem(me + t, devices), 0).wait_send()
        row_copy(lax.rem(me + t, devices), 1).start()

    @pl.when(partner != me)
    def _():
        place_copy.wait_recv()
        cent_copy.wait_recv()

    places = as_column(place_in[...].astype(jnp.float32))
    per_part = max(1, 256 // slots)

    def collect(h):
        for first in range(0, devices, per_part):
            for s in range(first, first + per_part):
                @pl.when(s != me)
                def _(s=s):
                    row_arrival(s, h).wait_recv()
            ids = (first * slots + iota((members, per_part * slots), 1)).astype(jnp.float32)
            pick = (places == ids).astype(jnp.float32).astype(jnp.bfloat16)
            base = h * devices + first
            found = dot_nn(pick, arrived[base:base + per_part].reshape(per_part * slots, part))
            if first == 0:
                total[h] = found
            else:
                total[h] += found

    block = lax.rem(partner, wide)
    cluster = lax.div(partner, wide)
    chips = wide // 2
    chip, core = lax.div(block, 2), lax.rem(block, 2)
    sibling = role(cluster * wide + 2 * chip + 1 - core)

    def block_copy(target_chip, h):
        at = h * wide + block
        return remote(gathered.at[at], gathered.at[at], block_send.at[h * chips + target_chip],
                      block_recv.at[at], role(cluster * wide + 2 * target_chip + core))

    def sibling_copy(which, h):
        at = h * wide + which
        return remote(gathered.at[at], gathered.at[at], pass_send.at[at], block_recv.at[at], sibling)

    def scale_copy(which, target):
        return remote(scales.at[which], scales.at[which], scale_send.at[target],
                      scale_recv.at[which], role(cluster * wide + target))

    def send_block(h):
        @pl.loop(chip + 1, chips)
        def _(later):
            block_copy(later, h).start()

        @pl.when(core == 0)
        def _():
            sibling_copy(block, h).start()

    collect(0)
    gathered[block] = total[0].astype(jnp.bfloat16)
    send_block(0)

    collect(1)
    left, right = total[0], total[1]
    squares = jnp.sum(left * left, axis=1, keepdims=True) + jnp.sum(right * right, axis=1, keepdims=True)
    scale = lax.rsqrt(squares + 1e-06)
    scales[block] = jnp.transpose(jnp.broadcast_to(scale, (members, LANES)))[:1]

    @pl.loop(block + 1, wide)
    def _(target):
        scale_copy(block, target).start()

    left, right = left * scale, right * scale
    gathered[wide + block] = right.astype(jnp.bfloat16)
    send_block(1)
    own[...] = left.astype(jnp.bfloat16)

    centroid = cent_in[...]
    direction = centroid * lax.rsqrt(jnp.sum(centroid * centroid, axis=1, keepdims=True) + 1e-06)
    distance = 1.0 - (
        jnp.sum(left * direction[:, :part], axis=1, keepdims=True)
        + jnp.sum(right * direction[:, part:], axis=1, keepdims=True)
    )

    def fold(scores):
        out = scores[:, :LANES]
        for i in range(1, members // LANES):
            out = jnp.maximum(out, scores[:, i * LANES:(i + 1) * LANES])
        return out

    mine = gathered[wide + block]
    scores = dot_nt(own[...], own[...]) + dot_nt(mine, mine)
    scores = jnp.where(iota((members, members), 1) < iota((members, members), 0), scores, -1.0)
    best[...] = jnp.maximum(fold(scores), -1.0)

    def meet(which):
        scale_copy(which, block).wait_recv()
        first_half = gathered[which].astype(jnp.float32) * as_column(scales[which])
        scores = dot_nt(own[...], first_half.astype(jnp.bfloat16))
        scores += dot_nt(gathered[wide + block], gathered[wide + which])
        best[...] = jnp.maximum(best[...], fold(scores))

    @pl.loop(0, chip)
    def _(t):
        direct = 2 * (chip - 1 - t) + core
        sibling_copy(direct, 0).wait_recv()
        sibling_copy(direct, 0).start()

    @pl.when(core == 1)
    def _():
        sibling_copy(2 * chip, 0).wait_recv()
        sibling_copy(2 * chip, 1).wait_recv()
        meet(2 * chip)

    @pl.loop(0, chip)
    def _(t):
        direct = 2 * (chip - 1 - t) + core
        sibling_copy(direct, 1).wait_recv()
        sibling_copy(direct, 1).start()
        meet(direct)
        passed = 2 * (chip - 1 - t) + 1 - core
        sibling_copy(passed, 0).wait_recv()
        sibling_copy(passed, 1).wait_recv()
        meet(passed)

    nearest = jnp.max(best[...], axis=1, keepdims=True)
    column = iota((members, LANES), 1)
    both = jnp.transpose(jnp.where(column == 0, nearest, distance))
    res_out[...] = both[:8]

    res_copy = remote(res_out, res_in, res_send, res_recv, partner)

    @pl.when(partner != me)
    def _():
        res_copy.start()
        res_copy.wait_recv()

    @pl.when(partner == me)
    def _():
        res_in[...] = res_out[...]

    near_ref[...] = res_in[0:1, :]
    dist_ref[...] = res_in[1:2, :]

    @pl.when(partner != me)
    def _():
        res_copy.wait_send()
        place_copy.wait_send()
        cent_copy.wait_send()

    @pl.loop(1, devices)
    def _(t):
        other = lax.rem(me + t, devices)
        remote(wanted.at[other], asked.at[me], ask_send.at[other], ask_recv.at[me], other).wait_send()
        row_copy(other, 1).wait_send()

    @pl.loop(chip + 1, chips)
    def _(later):
        block_copy(later, 0).wait_send()
        block_copy(later, 1).wait_send()

    @pl.when(core == 0)
    def _():
        sibling_copy(block, 0).wait_send()
        sibling_copy(block, 1).wait_send()

    @pl.loop(0, chip)
    def _(t):
        direct = 2 * (chip - 1 - t) + core
        sibling_copy(direct, 0).wait_send()
        sibling_copy(direct, 1).wait_send()

    @pl.loop(block + 1, wide)
    def _(target):
        scale_copy(block, target).wait_send()


def solution(mesh):
    clusters, wide = mesh.shape["clus"], mesh.shape["wide"]
    devices = clusters * wide

    def on_device(documents, source_device, source_row, centroids):
        members = source_device.shape[1]
        width = documents.shape[1]
        cap = 2 * members // devices
        slots = max(16, cap)
        dma = pltpu.SemaphoreType.DMA
        f32, bf16, i32 = jnp.float32, jnp.bfloat16, jnp.int32
        vmem = pl.BlockSpec(memory_space=pltpu.VMEM)
        return pl.pallas_call(
            functools.partial(kernel, clusters, wide, cap, slots),
            out_shape=[jax.ShapeDtypeStruct((1, members), f32)] * 2,
            in_specs=[vmem] * 4,
            out_specs=[vmem] * 2,
            scratch_shapes=[
                pltpu.VMEM((devices, 1, LANES), i32),
                pltpu.VMEM((devices, 1, LANES), i32),
                pltpu.VMEM((1, members), i32),
                pltpu.VMEM((1, members), i32),
                pltpu.VMEM((1, width), f32),
                pltpu.VMEM((1, width), f32),
                pltpu.VMEM((2 * devices, slots, width // 2), bf16),
                pltpu.VMEM((2 * devices, slots, width // 2), bf16),
                pltpu.VMEM((2, members, width // 2), f32),
                pltpu.VMEM((2 * wide, members, width // 2), bf16),
                pltpu.VMEM((members, width // 2), bf16),
                pltpu.VMEM((wide, 1, members), f32),
                pltpu.VMEM((members, LANES), f32),
                pltpu.VMEM((8, members), f32),
                pltpu.VMEM((8, members), f32),
                dma((devices,)), dma((devices,)), dma((2,)), dma((2,)),
                dma((2 * devices,)), dma((2 * devices,)),
                dma((wide,)), dma((2 * wide,)), dma((2 * wide,)),
                dma((wide,)), dma((wide,)), dma, dma,
            ],
            compiler_params=pltpu.CompilerParams(
                collective_id=0, has_side_effects=True, vmem_limit_bytes=56 * 1024 * 1024
            ),
        )(documents, source_device, source_row, centroids)

    placed = (P(("clus", "wide"), None), P("clus", "wide"), P("clus", "wide"), P("clus", None))
    return jax.shard_map(
        on_device,
        mesh=mesh,
        in_specs=placed,
        out_specs=(P("clus", "wide"), P("clus", "wide")),
        check_vma=False,
    )
```

```python
import functools

import jax
import jax.numpy as jnp
from jax import lax
from jax.experimental import pallas as pl
from jax.experimental.pallas import tpu as pltpu
from jax.sharding import PartitionSpec as P

MESH = pl.DeviceIdType.MESH
LANES = 128


def iota(shape, dim):
    return lax.broadcasted_iota(jnp.int32, shape, dim)


def dot_nt(left, right):
    return lax.dot_general(
        left, right, (((1,), (1,)), ((), ())), preferred_element_type=jnp.float32
    )


def dot_nn(left, right):
    return jnp.dot(left, right, preferred_element_type=jnp.float32)


def as_column(row):
    return jnp.transpose(jnp.broadcast_to(row, (LANES, row.shape[1])))[:, :1]


def kernel(
    clusters, wide, cap, slots,
    docs_ref, sender_ref, row_ref, centroid_ref,
    near_ref, dist_ref,
    wanted, asked, place_out, place_in, cent_out, cent_in,
    outgoing, arrived, total, gathered, own, scales, best, res_out, res_in,
    ask_send, ask_recv, info_send, info_recv, row_send, row_recv,
    block_send, block_recv, pass_send, scale_send, scale_recv, res_send, res_recv,
):
    devices = clusters * wide
    members = sender_ref.shape[1]
    doc_rows, width = docs_ref.shape
    part = width // 2
    swapped = wide == 2 * clusters
    my_clus = lax.axis_index("clus")
    my_wide = lax.axis_index("wide")
    me = my_clus * wide + my_wide

    def role(device):
        if not swapped:
            return device
        first, rest = lax.div(device, wide), lax.rem(device, wide)
        return lax.div(rest, 2) * wide + 2 * first + lax.rem(rest, 2)

    def where_is(device):
        return (lax.div(device, wide), lax.rem(device, wide))

    def remote(src, dst, send, recv, device):
        return pltpu.make_async_remote_copy(
            src_ref=src, dst_ref=dst, send_sem=send, recv_sem=recv,
            device_id=where_is(device), device_id_type=MESH,
        )

    barrier = pltpu.get_barrier_semaphore()

    @pl.loop(1, devices)
    def _(t):
        other = lax.rem(me + t, devices)
        pl.semaphore_signal(barrier, inc=1, device_id=where_is(other), device_id_type=MESH)

    senders = sender_ref[...]
    same = iota((devices, members), 0) == senders
    one_hot = same.astype(jnp.float32)
    earlier = (iota((members, members), 0) < iota((members, members), 1)).astype(jnp.float32)
    rank = dot_nn(one_hot.astype(jnp.bfloat16), earlier.astype(jnp.bfloat16))
    slot = jnp.sum(jnp.where(same, rank, 0.0), axis=0, keepdims=True).astype(jnp.int32)
    place_out[...] = senders * slots + slot
    cent_out[...] = centroid_ref[...]
    at_slot = (iota((LANES, members), 0) == slot).astype(jnp.float32).astype(jnp.bfloat16)
    named = row_ref[...] + 1
    high = lax.shift_right_logical(named, 8)
    low = named - high * 256
    ask_low = dot_nt((one_hot * low.astype(jnp.float32)).astype(jnp.bfloat16), at_slot)
    ask_high = dot_nt((one_hot * high.astype(jnp.float32)).astype(jnp.bfloat16), at_slot)
    ask = (ask_low + 256.0 * ask_high).astype(jnp.int32)
    for s in range(devices):
        wanted[s] = ask[s:s + 1, :]

    pl.semaphore_wait(barrier, devices - 1)

    partner = role(me)
    asked[me] = wanted[me]

    @pl.loop(1, devices)
    def _(t):
        other = lax.rem(me + t, devices)
        remote(wanted.at[other], asked.at[me], ask_send.at[other], ask_recv.at[me], other).start()

    place_copy = remote(place_out, place_in, info_send.at[0], info_recv.at[0], partner)
    cent_copy = remote(cent_out, cent_in, info_send.at[1], info_recv.at[1], partner)

    @pl.when(partner != me)
    def _():
        place_copy.start()
        cent_copy.start()

    @pl.when(partner == me)
    def _():
        place_in[...] = place_out[...]
        cent_in[...] = cent_out[...]

    @pl.loop(1, devices)
    def _(t):
        other = lax.rem(me + devices - t, devices)
        remote(wanted.at[me], asked.at[other], ask_send.at[other], ask_recv.at[other], other).wait_recv()

    asked_t = jnp.transpose(asked[:, 0, :].astype(jnp.float32))
    doc_ids = (iota((slots, doc_rows), 1) + 1).astype(jnp.float32)
    docs = docs_ref[...]
    per_dot = max(1, LANES // slots)
    for first in range(0, devices, per_dot):
        chosen = jnp.concatenate(
            [
                (asked_t[:slots, o:o + 1] == doc_ids).astype(jnp.float32)
                for o in range(first, first + per_dot)
            ],
            axis=0,
        ).astype(jnp.bfloat16)
        rows = dot_nn(chosen, docs).astype(jnp.bfloat16)
        for i in range(per_dot):
            outgoing[first + i] = rows[i * slots:(i + 1) * slots, :part]
            outgoing[devices + first + i] = rows[i * slots:(i + 1) * slots, part:]

    def row_copy(holder, h):
        return remote(outgoing.at[h * devices + role(holder)], arrived.at[h * devices + me],
                      row_send.at[h * devices + holder], row_recv.at[h * devices + me], holder)

    def row_arrival(source, h):
        at = h * devices + source
        return remote(outgoing.at[at], arrived.at[at], row_send.at[at], row_recv.at[at], source)

    stride = 5 if devices % 5 else 1

    @pl.loop(1, devices)
    def _(t):
        row_copy(lax.rem(me + stride * t, devices), 0).start()

    arrived[me] = outgoing[partner]
    arrived[devices + me] = outgoing[devices + partner]

    @pl.loop(1, devices)
    def _(t):
        row_copy(lax.rem(me + stride * t, devices), 0).wait_send()
        row_copy(lax.rem(me + stride * t, devices), 1).start()

    @pl.when(partner != me)
    def _():
        place_copy.wait_recv()
        cent_copy.wait_recv()

    places = as_column(place_in[...].astype(jnp.float32))
    per_part = max(1, 256 // slots)

    def collect(h):
        for first in range(0, devices, per_part):
            for s in range(first, first + per_part):
                @pl.when(s != me)
                def _(s=s):
                    row_arrival(s, h).wait_recv()
            ids = (first * slots + iota((members, per_part * slots), 1)).astype(jnp.float32)
            pick = (places == ids).astype(jnp.float32).astype(jnp.bfloat16)
            base = h * devices + first
            found = dot_nn(pick, arrived[base:base + per_part].reshape(per_part * slots, part))
            if first == 0:
                total[h] = found
            else:
                total[h] += found

    block = lax.rem(partner, wide)
    cluster = lax.div(partner, wide)
    chips = wide // 2
    chip, core = lax.div(block, 2), lax.rem(block, 2)
    sibling = role(cluster * wide + 2 * chip + 1 - core)

    def block_copy(target_chip, h):
        at = h * wide + block
        return remote(gathered.at[at], gathered.at[at], block_send.at[h * chips + target_chip],
                      block_recv.at[at], role(cluster * wide + 2 * target_chip + core))

    def sibling_copy(which, h):
        at = h * wide + which
        return remote(gathered.at[at], gathered.at[at], pass_send.at[at], block_recv.at[at], sibling)

    def scale_copy(which, target):
        return remote(scales.at[which], scales.at[which], scale_send.at[target],
                      scale_recv.at[which], role(cluster * wide + target))

    def send_block(h):
        @pl.loop(chip + 1, chips)
        def _(later):
            block_copy(later, h).start()

        @pl.when(core == 0)
        def _():
            sibling_copy(block, h).start()

    collect(0)
    gathered[block] = total[0].astype(jnp.bfloat16)
    send_block(0)

    collect(1)
    left, right = total[0], total[1]
    squares = jnp.sum(left * left, axis=1, keepdims=True) + jnp.sum(right * right, axis=1, keepdims=True)
    scale = lax.rsqrt(squares + 1e-06)
    scales[block] = jnp.transpose(jnp.broadcast_to(scale, (members, LANES)))[:1]

    @pl.loop(block + 1, wide)
    def _(target):
        scale_copy(block, target).start()

    left, right = left * scale, right * scale
    gathered[wide + block] = right.astype(jnp.bfloat16)
    send_block(1)
    own[...] = left.astype(jnp.bfloat16)

    centroid = cent_in[...]
    direction = centroid * lax.rsqrt(jnp.sum(centroid * centroid, axis=1, keepdims=True) + 1e-06)
    distance = 1.0 - (
        jnp.sum(left * direction[:, :part], axis=1, keepdims=True)
        + jnp.sum(right * direction[:, part:], axis=1, keepdims=True)
    )

    def fold(scores):
        out = scores[:, :LANES]
        for i in range(1, members // LANES):
            out = jnp.maximum(out, scores[:, i * LANES:(i + 1) * LANES])
        return out

    mine = gathered[wide + block]
    scores = dot_nt(own[...], own[...]) + dot_nt(mine, mine)
    scores = jnp.where(iota((members, members), 1) < iota((members, members), 0), scores, -1.0)
    best[...] = jnp.maximum(fold(scores), -1.0)

    def meet(which):
        scale_copy(which, block).wait_recv()
        first_half = gathered[which].astype(jnp.float32) * as_column(scales[which])
        scores = dot_nt(own[...], first_half.astype(jnp.bfloat16))
        scores += dot_nt(gathered[wide + block], gathered[wide + which])
        best[...] = jnp.maximum(best[...], fold(scores))

    @pl.loop(0, chip)
    def _(t):
        direct = 2 * (chip - 1 - t) + core
        sibling_copy(direct, 0).wait_recv()
        sibling_copy(direct, 0).start()

    @pl.when(core == 1)
    def _():
        sibling_copy(2 * chip, 0).wait_recv()
        sibling_copy(2 * chip, 1).wait_recv()
        meet(2 * chip)

    @pl.loop(0, chip)
    def _(t):
        direct = 2 * (chip - 1 - t) + core
        sibling_copy(direct, 1).wait_recv()
        sibling_copy(direct, 1).start()
        meet(direct)
        passed = 2 * (chip - 1 - t) + 1 - core
        sibling_copy(passed, 0).wait_recv()
        sibling_copy(passed, 1).wait_recv()
        meet(passed)

    nearest = jnp.max(best[...], axis=1, keepdims=True)
    column = iota((members, LANES), 1)
    both = jnp.transpose(jnp.where(column == 0, nearest, distance))
    res_out[...] = both[:8]

    res_copy = remote(res_out, res_in, res_send, res_recv, partner)

    @pl.when(partner != me)
    def _():
        res_copy.start()
        res_copy.wait_recv()

    @pl.when(partner == me)
    def _():
        res_in[...] = res_out[...]

    near_ref[...] = res_in[0:1, :]
    dist_ref[...] = res_in[1:2, :]

    @pl.when(partner != me)
    def _():
        res_copy.wait_send()
        place_copy.wait_send()
        cent_copy.wait_send()

    @pl.loop(1, devices)
    def _(t):
        other = lax.rem(me + t, devices)
        remote(wanted.at[other], asked.at[me], ask_send.at[other], ask_recv.at[me], other).wait_send()
        row_copy(other, 1).wait_send()

    @pl.loop(chip + 1, chips)
    def _(later):
        block_copy(later, 0).wait_send()
        block_copy(later, 1).wait_send()

    @pl.when(core == 0)
    def _():
        sibling_copy(block, 0).wait_send()
        sibling_copy(block, 1).wait_send()

    @pl.loop(0, chip)
    def _(t):
        direct = 2 * (chip - 1 - t) + core
        sibling_copy(direct, 0).wait_send()
        sibling_copy(direct, 1).wait_send()

    @pl.loop(block + 1, wide)
    def _(target):
        scale_copy(block, target).wait_send()


def solution(mesh):
    clusters, wide = mesh.shape["clus"], mesh.shape["wide"]
    devices = clusters * wide

    def on_device(documents, source_device, source_row, centroids):
        members = source_device.shape[1]
        width = documents.shape[1]
        cap = 2 * members // devices
        slots = max(16, cap)
        dma = pltpu.SemaphoreType.DMA
        f32, bf16, i32 = jnp.float32, jnp.bfloat16, jnp.int32
        vmem = pl.BlockSpec(memory_space=pltpu.VMEM)
        return pl.pallas_call(
            functools.partial(kernel, clusters, wide, cap, slots),
            out_shape=[jax.ShapeDtypeStruct((1, members), f32)] * 2,
            in_specs=[vmem] * 4,
            out_specs=[vmem] * 2,
            scratch_shapes=[
                pltpu.VMEM((devices, 1, LANES), i32),
                pltpu.VMEM((devices, 1, LANES), i32),
                pltpu.VMEM((1, members), i32),
                pltpu.VMEM((1, members), i32),
                pltpu.VMEM((1, width), f32),
                pltpu.VMEM((1, width), f32),
                pltpu.VMEM((2 * devices, slots, width // 2), bf16),
                pltpu.VMEM((2 * devices, slots, width // 2), bf16),
                pltpu.VMEM((2, members, width // 2), f32),
                pltpu.VMEM((2 * wide, members, width // 2), bf16),
                pltpu.VMEM((members, width // 2), bf16),
                pltpu.VMEM((wide, 1, members), f32),
                pltpu.VMEM((members, LANES), f32),
                pltpu.VMEM((8, members), f32),
                pltpu.VMEM((8, members), f32),
                dma((devices,)), dma((devices,)), dma((2,)), dma((2,)),
                dma((2 * devices,)), dma((2 * devices,)),
                dma((wide,)), dma((2 * wide,)), dma((2 * wide,)),
                dma((wide,)), dma((wide,)), dma, dma,
            ],
            compiler_params=pltpu.CompilerParams(
                collective_id=0, has_side_effects=True, vmem_limit_bytes=56 * 1024 * 1024
            ),
        )(documents, source_device, source_row, centroids)

    placed = (P(("clus", "wide"), None), P("clus", "wide"), P("clus", "wide"), P("clus", None))
    return jax.shard_map(
        on_device,
        mesh=mesh,
        in_specs=placed,
        out_specs=(P("clus", "wide"), P("clus", "wide")),
        check_vma=False,
    )
```

```python
import functools

import jax
import jax.numpy as jnp
from jax import lax
from jax.experimental import pallas as pl
from jax.experimental.pallas import tpu as pltpu
from jax.sharding import PartitionSpec as P

MESH = pl.DeviceIdType.MESH
LANES = 128


def iota(shape, dim):
    return lax.broadcasted_iota(jnp.int32, shape, dim)


def dot_nt(left, right):
    return lax.dot_general(
        left, right, (((1,), (1,)), ((), ())), preferred_element_type=jnp.float32
    )


def dot_nn(left, right):
    return jnp.dot(left, right, preferred_element_type=jnp.float32)


def as_column(row):
    return jnp.transpose(jnp.broadcast_to(row, (LANES, row.shape[1])))[:, :1]


def kernel(
    clusters, wide, cap, slots,
    docs_ref, sender_ref, row_ref, centroid_ref,
    near_ref, dist_ref,
    wanted, asked, place_out, place_in, cent_out, cent_in,
    outgoing, arrived, total, gathered, own, scales, best, res_out, res_in,
    ask_send, ask_recv, info_send, info_recv, row_send, row_recv,
    block_send, block_recv, pass_send, scale_send, scale_recv, res_send, res_recv,
):
    devices = clusters * wide
    members = sender_ref.shape[1]
    doc_rows, width = docs_ref.shape
    part = width // 2
    swapped = wide == 2 * clusters
    my_clus = lax.axis_index("clus")
    my_wide = lax.axis_index("wide")
    me = my_clus * wide + my_wide

    def role(device):
        if not swapped:
            return device
        first, rest = lax.div(device, wide), lax.rem(device, wide)
        return lax.div(rest, 2) * wide + 2 * first + lax.rem(rest, 2)

    def where_is(device):
        return (lax.div(device, wide), lax.rem(device, wide))

    def remote(src, dst, send, recv, device):
        return pltpu.make_async_remote_copy(
            src_ref=src, dst_ref=dst, send_sem=send, recv_sem=recv,
            device_id=where_is(device), device_id_type=MESH,
        )

    barrier = pltpu.get_barrier_semaphore()

    @pl.loop(1, devices)
    def _(t):
        other = lax.rem(me + t, devices)
        pl.semaphore_signal(barrier, inc=1, device_id=where_is(other), device_id_type=MESH)

    senders = sender_ref[...]
    same = iota((devices, members), 0) == senders
    one_hot = same.astype(jnp.float32)
    earlier = (iota((members, members), 0) < iota((members, members), 1)).astype(jnp.float32)
    rank = dot_nn(one_hot.astype(jnp.bfloat16), earlier.astype(jnp.bfloat16))
    slot = jnp.sum(jnp.where(same, rank, 0.0), axis=0, keepdims=True).astype(jnp.int32)
    place_out[...] = senders * slots + slot
    cent_out[...] = centroid_ref[...]
    at_slot = (iota((LANES, members), 0) == slot).astype(jnp.float32).astype(jnp.bfloat16)
    named = row_ref[...] + 1
    high = lax.shift_right_logical(named, 8)
    low = named - high * 256
    ask_low = dot_nt((one_hot * low.astype(jnp.float32)).astype(jnp.bfloat16), at_slot)
    ask_high = dot_nt((one_hot * high.astype(jnp.float32)).astype(jnp.bfloat16), at_slot)
    ask = (ask_low + 256.0 * ask_high).astype(jnp.int32)
    for s in range(devices):
        wanted[s] = ask[s:s + 1, :]

    pl.semaphore_wait(barrier, devices - 1)

    partner = role(me)
    asked[me] = wanted[me]

    @pl.loop(1, devices)
    def _(t):
        other = lax.rem(me + t, devices)
        remote(wanted.at[other], asked.at[me], ask_send.at[other], ask_recv.at[me], other).start()

    place_copy = remote(place_out, place_in, info_send.at[0], info_recv.at[0], partner)
    cent_copy = remote(cent_out, cent_in, info_send.at[1], info_recv.at[1], partner)

    @pl.when(partner != me)
    def _():
        place_copy.start()
        cent_copy.start()

    @pl.when(partner == me)
    def _():
        place_in[...] = place_out[...]
        cent_in[...] = cent_out[...]

    @pl.loop(1, devices)
    def _(t):
        other = lax.rem(me + devices - t, devices)
        remote(wanted.at[me], asked.at[other], ask_send.at[other], ask_recv.at[other], other).wait_recv()

    asked_t = jnp.transpose(asked[:, 0, :].astype(jnp.float32))
    doc_ids = (iota((slots, doc_rows), 1) + 1).astype(jnp.float32)
    docs = docs_ref[...]
    per_dot = max(1, LANES // slots)
    for first in range(0, devices, per_dot):
        chosen = jnp.concatenate(
            [
                (asked_t[:slots, o:o + 1] == doc_ids).astype(jnp.float32)
                for o in range(first, first + per_dot)
            ],
            axis=0,
        ).astype(jnp.bfloat16)
        rows = dot_nn(chosen, docs).astype(jnp.bfloat16)
        for i in range(per_dot):
            outgoing[first + i] = rows[i * slots:(i + 1) * slots, :part]
            outgoing[devices + first + i] = rows[i * slots:(i + 1) * slots, part:]

    def row_copy(holder, h):
        return remote(outgoing.at[h * devices + role(holder)], arrived.at[h * devices + me],
                      row_send.at[h * devices + holder], row_recv.at[h * devices + me], holder)

    def row_arrival(source, h):
        at = h * devices + source
        return remote(outgoing.at[at], arrived.at[at], row_send.at[at], row_recv.at[at], source)

    stride = 5 if devices % 5 else 1

    @pl.loop(1, devices)
    def _(t):
        row_copy(lax.rem(me + stride * t, devices), 0).start()

    arrived[me] = outgoing[partner]
    arrived[devices + me] = outgoing[devices + partner]

    @pl.loop(1, devices)
    def _(t):
        row_copy(lax.rem(me + stride * t, devices), 1).start()

    @pl.when(partner != me)
    def _():
        place_copy.wait_recv()
        cent_copy.wait_recv()

    places = as_column(place_in[...].astype(jnp.float32))
    per_part = max(1, 256 // slots)

    def collect(h):
        for first in range(0, devices, per_part):
            for s in range(first, first + per_part):
                @pl.when(s != me)
                def _(s=s):
                    row_arrival(s, h).wait_recv()
            ids = (first * slots + iota((members, per_part * slots), 1)).astype(jnp.float32)
            pick = (places == ids).astype(jnp.float32).astype(jnp.bfloat16)
            base = h * devices + first
            found = dot_nn(pick, arrived[base:base + per_part].reshape(per_part * slots, part))
            if first == 0:
                total[h] = found
            else:
                total[h] += found

    block = lax.rem(partner, wide)
    cluster = lax.div(partner, wide)
    chips = wide // 2
    chip, core = lax.div(block, 2), lax.rem(block, 2)
    sibling = role(cluster * wide + 2 * chip + 1 - core)

    def block_copy(target_chip, h):
        at = h * wide + block
        return remote(gathered.at[at], gathered.at[at], block_send.at[h * chips + target_chip],
                      block_recv.at[at], role(cluster * wide + 2 * target_chip + core))

    def sibling_copy(which, h):
        at = h * wide + which
        return remote(gathered.at[at], gathered.at[at], pass_send.at[at], block_recv.at[at], sibling)

    def scale_copy(which, target):
        return remote(scales.at[which], scales.at[which], scale_send.at[target],
                      scale_recv.at[which], role(cluster * wide + target))

    def send_block(h):
        @pl.loop(chip + 1, chips)
        def _(later):
            block_copy(chips + chip - later, h).start()

        @pl.when(core == 0)
        def _():
            sibling_copy(block, h).start()

    collect(0)
    gathered[block] = total[0].astype(jnp.bfloat16)
    send_block(0)

    collect(1)
    left, right = total[0], total[1]
    squares = jnp.sum(left * left, axis=1, keepdims=True) + jnp.sum(right * right, axis=1, keepdims=True)
    scale = lax.rsqrt(squares + 1e-06)
    scales[block] = jnp.transpose(jnp.broadcast_to(scale, (members, LANES)))[:1]

    @pl.loop(block + 1, wide)
    def _(target):
        scale_copy(block, target).start()

    left, right = left * scale, right * scale
    gathered[wide + block] = right.astype(jnp.bfloat16)
    send_block(1)
    own[...] = left.astype(jnp.bfloat16)

    centroid = cent_in[...]
    direction = centroid * lax.rsqrt(jnp.sum(centroid * centroid, axis=1, keepdims=True) + 1e-06)
    distance = 1.0 - (
        jnp.sum(left * direction[:, :part], axis=1, keepdims=True)
        + jnp.sum(right * direction[:, part:], axis=1, keepdims=True)
    )

    def fold(scores):
        out = scores[:, :LANES]
        for i in range(1, members // LANES):
            out = jnp.maximum(out, scores[:, i * LANES:(i + 1) * LANES])
        return out

    mine = gathered[wide + block]
    scores = dot_nt(own[...], own[...]) + dot_nt(mine, mine)
    scores = jnp.where(iota((members, members), 1) < iota((members, members), 0), scores, -1.0)
    best[...] = jnp.maximum(fold(scores), -1.0)

    def meet(which):
        scale_copy(which, block).wait_recv()
        first_half = gathered[which].astype(jnp.float32) * as_column(scales[which])
        scores = dot_nt(own[...], first_half.astype(jnp.bfloat16))
        scores += dot_nt(gathered[wide + block], gathered[wide + which])
        best[...] = jnp.maximum(best[...], fold(scores))

    @pl.loop(0, chip)
    def _(t):
        direct = 2 * (chip - 1 - t) + core
        sibling_copy(direct, 0).wait_recv()
        sibling_copy(direct, 0).start()

    @pl.when(core == 1)
    def _():
        sibling_copy(2 * chip, 0).wait_recv()
        sibling_copy(2 * chip, 1).wait_recv()
        meet(2 * chip)

    @pl.loop(0, chip)
    def _(t):
        direct = 2 * (chip - 1 - t) + core
        sibling_copy(direct, 1).wait_recv()
        sibling_copy(direct, 1).start()
        meet(direct)
        passed = 2 * (chip - 1 - t) + 1 - core
        sibling_copy(passed, 0).wait_recv()
        sibling_copy(passed, 1).wait_recv()
        meet(passed)

    nearest = jnp.max(best[...], axis=1, keepdims=True)
    column = iota((members, LANES), 1)
    both = jnp.transpose(jnp.where(column == 0, nearest, distance))
    res_out[...] = both[:8]

    res_copy = remote(res_out, res_in, res_send, res_recv, partner)

    @pl.when(partner != me)
    def _():
        res_copy.start()
        res_copy.wait_recv()

    @pl.when(partner == me)
    def _():
        res_in[...] = res_out[...]

    near_ref[...] = res_in[0:1, :]
    dist_ref[...] = res_in[1:2, :]

    @pl.when(partner != me)
    def _():
        res_copy.wait_send()
        place_copy.wait_send()
        cent_copy.wait_send()

    @pl.loop(1, devices)
    def _(t):
        other = lax.rem(me + t, devices)
        remote(wanted.at[other], asked.at[me], ask_send.at[other], ask_recv.at[me], other).wait_send()
        row_copy(other, 0).wait_send()
        row_copy(other, 1).wait_send()

    @pl.loop(chip + 1, chips)
    def _(later):
        block_copy(later, 0).wait_send()
        block_copy(later, 1).wait_send()

    @pl.when(core == 0)
    def _():
        sibling_copy(block, 0).wait_send()
        sibling_copy(block, 1).wait_send()

    @pl.loop(0, chip)
    def _(t):
        direct = 2 * (chip - 1 - t) + core
        sibling_copy(direct, 0).wait_send()
        sibling_copy(direct, 1).wait_send()

    @pl.loop(block + 1, wide)
    def _(target):
        scale_copy(block, target).wait_send()


def solution(mesh):
    clusters, wide = mesh.shape["clus"], mesh.shape["wide"]
    devices = clusters * wide

    def on_device(documents, source_device, source_row, centroids):
        members = source_device.shape[1]
        width = documents.shape[1]
        cap = 2 * members // devices
        slots = max(16, cap)
        dma = pltpu.SemaphoreType.DMA
        f32, bf16, i32 = jnp.float32, jnp.bfloat16, jnp.int32
        vmem = pl.BlockSpec(memory_space=pltpu.VMEM)
        return pl.pallas_call(
            functools.partial(kernel, clusters, wide, cap, slots),
            out_shape=[jax.ShapeDtypeStruct((1, members), f32)] * 2,
            in_specs=[vmem] * 4,
            out_specs=[vmem] * 2,
            scratch_shapes=[
                pltpu.VMEM((devices, 1, LANES), i32),
                pltpu.VMEM((devices, 1, LANES), i32),
                pltpu.VMEM((1, members), i32),
                pltpu.VMEM((1, members), i32),
                pltpu.VMEM((1, width), f32),
                pltpu.VMEM((1, width), f32),
                pltpu.VMEM((2 * devices, slots, width // 2), bf16),
                pltpu.VMEM((2 * devices, slots, width // 2), bf16),
                pltpu.VMEM((2, members, width // 2), f32),
                pltpu.VMEM((2 * wide, members, width // 2), bf16),
                pltpu.VMEM((members, width // 2), bf16),
                pltpu.VMEM((wide, 1, members), f32),
                pltpu.VMEM((members, LANES), f32),
                pltpu.VMEM((8, members), f32),
                pltpu.VMEM((8, members), f32),
                dma((devices,)), dma((devices,)), dma((2,)), dma((2,)),
                dma((2 * devices,)), dma((2 * devices,)),
                dma((wide,)), dma((2 * wide,)), dma((2 * wide,)),
                dma((wide,)), dma((wide,)), dma, dma,
            ],
            compiler_params=pltpu.CompilerParams(
                collective_id=0, has_side_effects=True, vmem_limit_bytes=56 * 1024 * 1024
            ),
        )(documents, source_device, source_row, centroids)

    placed = (P(("clus", "wide"), None), P("clus", "wide"), P("clus", "wide"), P("clus", None))
    return jax.shard_map(
        on_device,
        mesh=mesh,
        in_specs=placed,
        out_specs=(P("clus", "wide"), P("clus", "wide")),
        check_vma=False,
    )
```
